256 devices in a mesh: tm: 16 (over z, y_hi), rows: 16 (over y_lo, x, core).
Axes of the slice: x: 4, y: 4 (y_hi: 2, y_lo: 2; y = y_hi * 2 + y_lo), z: 8, core: 2. Of those that a mesh axis runs over, the one named last changes fastest.
Arguments:
- features: bfloat16 [64, 128, 512, 128], P('tm', 'rows'), may hold values from -6 to 6
- decoder_weight: bfloat16 [3, 3, 3, 128, 128], replicated, may hold values from -0.109375 to 0.109375
- decoder_bias: float32 [128], replicated, may hold values from -3 to 3
- critic_weight: bfloat16 [3, 3, 3, 128, 256], replicated, may hold values from -0.109375 to 0.109375
- critic_bias: float32 [256], replicated, may hold values from -3 to 3
Outputs:
- decoded: bfloat16 [64, 128, 512, 128], P('tm', 'rows')
- critic_features: bfloat16 [32, 64, 256, 256], P('tm', 'rows')
The draws below stay inside these ranges and needn't reach their ends.
All inputs are finite; a program needn't handle non-finite values.
Results may differ from the reference program's by a relative error of at most 0.0049.
Values may be sent and summed in bfloat16 or wider, within the bound.
A program may use at most 128 MiB of HBM per device.

```python
import jax
import jax.numpy as jnp
from jax import lax

C = 128
DC = 256
COLS = 512
FRAMES = 64
HEIGHT = 128


def block_levels(own_key, dims, split, least, top_value):
    loudness = 1.0
    for dim, shards_of in split:
        draws = jax.random.uniform(jax.random.fold_in(jax.random.fold_in(own_key, 6), dim), (shards_of,), jnp.float32, least / len(split), top_value / len(split))
        loudness = loudness * jnp.repeat(jnp.exp(draws), dims[dim] // shards_of).reshape((-1,) + (1,) * (len(dims) - 1 - dim))
    return loudness


def normal_values(key, shape, scale, reach, pieces=(), kind=jnp.bfloat16):
    factor_of = block_levels(key, shape, pieces, -0.22, 0.18) if pieces else 1.0
    values = jax.random.normal(key, shape, jnp.float32) * scale * factor_of
    return jnp.minimum(jnp.maximum(values, -reach), reach).astype(kind)


def setup_inputs(seed: int = 0) -> dict:
    key_list = jax.random.split(jax.random.key(seed), 6)
    return {
        "features": normal_values(key_list[0], (FRAMES, HEIGHT, COLS, C), 1.0, 6.0, ((0, 16), (1, 16))),
        "decoder_weight": normal_values(key_list[1], (3, 3, 3, C, C), (27 * C) ** -0.5, 0.109375),
        "decoder_bias": normal_values(key_list[2], (C,), 0.5, 3.0, (), jnp.float32),
        "critic_weight": normal_values(key_list[3], (3, 3, 3, C, DC), (27 * C) ** -0.5, 0.109375),
        "critic_bias": normal_values(key_list[4], (DC,), 0.5, 3.0, (), jnp.float32),
    }


def reference(features, decoder_weight, decoder_bias, critic_weight, critic_bias):
    frames, height, width, channels = features.shape
    activated = jax.nn.silu(features.astype(jnp.float32)).astype(jnp.bfloat16)
    padded = jnp.pad(activated, ((2, 0), (1, 1), (1, 1), (0, 0)))

    def decode_frame(frame):
        window = lax.dynamic_slice_in_dim(padded, frame, 3, 0)
        total = jnp.zeros((height * width, channels), jnp.float32)
        for tap_time in range(3):
            for tap_row in range(3):
                for tap_col in range(3):
                    piece = window[tap_time, tap_row:tap_row + height, tap_col:tap_col + width].reshape(-1, channels)
                    total = total + jnp.dot(piece, decoder_weight[tap_time, tap_row, tap_col], preferred_element_type=jnp.float32)
        residual = lax.dynamic_index_in_dim(features, frame, 0, keepdims=False).astype(jnp.float32).reshape(-1, channels)
        return (residual + total + decoder_bias.astype(jnp.float32)).astype(jnp.bfloat16).reshape(height, width, channels)

    decoded = lax.map(decode_frame, jnp.arange(frames, dtype=jnp.int32))
    critic_pad = jnp.pad(decoded, ((1, 0), (1, 0), (1, 0), (0, 0)))

    def critic_frame(index):
        window = lax.dynamic_slice_in_dim(critic_pad, 2 * index, 3, 0)
        total = jnp.zeros(((height // 2) * (width // 2), critic_weight.shape[-1]), jnp.float32)
        for tap_time in range(3):
            for tap_row in range(3):
                for tap_col in range(3):
                    piece = window[tap_time, tap_row:tap_row + height:2, tap_col:tap_col + width:2].reshape(-1, channels)
                    total = total + jnp.dot(piece, critic_weight[tap_time, tap_row, tap_col], preferred_element_type=jnp.float32)
        result = total + critic_bias.astype(jnp.float32)
        result = jnp.where(result > 0, result, 0.2 * result)
        return result.astype(jnp.bfloat16).reshape(height // 2, width // 2, -1)

    critic_features = lax.map(critic_frame, jnp.arange(frames // 2, dtype=jnp.int32))
    return decoded, critic_features
```

```python
import jax
import jax.numpy as jnp
from jax import lax
from jax.experimental import pallas as pl
from jax.experimental.pallas import tpu as pltpu
from jax.sharding import PartitionSpec as P

MESH = pl.DeviceIdType.MESH
BF = jnp.bfloat16
F32 = jnp.float32
ORDER = (7, 0, 6, 5, 4, 3, 2, 1)


def kernel(feat, w, db, cw, cb, out, cout,
           fv, act, wt, cwv, dbv, cbv, dec, cact, dech, part, cacc, qout, qin, co, scr,
           loc, osem, csem, tms, tmr, qs, qr, ups, upr, dns, dnr):
    tm = lax.axis_index("tm")
    row = lax.axis_index("rows")
    n_tm = lax.axis_size("tm")
    n_row = lax.axis_size("rows")
    has_next = tm < n_tm - 1
    has_prev = tm > 0
    has_up = row < n_row - 1
    has_dn = row > 0
    nxt = (lax.rem(tm + 1, n_tm), row)
    prv = (lax.rem(tm + n_tm - 1, n_tm), row)
    up = (tm, lax.rem(row + 1, n_row))
    dn = (tm, lax.rem(row + n_row - 1, n_row))

    local = [
        pltpu.make_async_copy(feat, fv.at[pl.ds(2, 4), pl.ds(1, 8)], loc.at[0]),
        pltpu.make_async_copy(cw, cwv, loc.at[1]),
        pltpu.make_async_copy(w, wt.at[:, pl.ds(0, 1152), pl.ds(0, 128)], loc.at[2]),
        pltpu.make_async_copy(w, wt.at[:, pl.ds(384, 1152), pl.ds(128, 128)], loc.at[3]),
        pltpu.make_async_copy(db, dbv, loc.at[4]),
        pltpu.make_async_copy(cb, cbv, loc.at[5]),
    ]
    for c in local:
        c.start()

    barrier = pltpu.get_barrier_semaphore()
    count = 0
    for ok, dev in ((has_next, nxt), (has_prev, prv), (has_up, up), (has_dn, dn)):
        @pl.when(ok)
        def _():
            pl.semaphore_signal(barrier, inc=1, device_id=dev, device_id_type=MESH)
        count = count + ok.astype(jnp.int32)
    pl.semaphore_wait(barrier, count)

    def remote(src, dst, ss, rs, dev):
        return pltpu.make_async_remote_copy(
            src_ref=src, dst_ref=dst, send_sem=ss, recv_sem=rs, device_id=dev, device_id_type=MESH)

    feats = [remote(feat.at[pl.ds(2, 2), h], fv.at[pl.ds(0, 2), h + 1], tms.at[k], tmr.at[k], nxt)
             for k, h in enumerate(ORDER)]
    own_up = remote(feat.at[:, 7], fv.at[pl.ds(2, 4), 0], ups.at[0], upr.at[0], up)
    own_dn = remote(feat.at[:, 0], fv.at[pl.ds(2, 4), 9], dns.at[0], dnr.at[0], dn)
    fwd_up = remote(fv.at[pl.ds(0, 2), 8], fv.at[pl.ds(0, 2), 0], ups.at[1], upr.at[1], up)
    fwd_dn = remote(fv.at[pl.ds(0, 2), 1], fv.at[pl.ds(0, 2), 9], dns.at[1], dnr.at[1], dn)
    decs = [remote(dec.at[f, 7], dech.at[f], ups.at[2 + f], upr.at[2 + f], up) for f in range(4)]
    quot = [remote(qout.at[j], qin.at[j], qs.at[j], qr.at[j], nxt) for j in range(4)]

    @pl.when(has_up)
    def _():
        own_up.start()

    @pl.when(has_dn)
    def _():
        own_dn.start()

    @pl.when(has_next)
    def _():
        for c in feats:
            c.start()

    zrow = jnp.zeros((512, 128), BF)

    @pl.when(jnp.logical_not(has_dn))
    def _():
        @pl.loop(0, 6)
        def _(f):
            fv[f, 0] = zrow

        @pl.loop(0, 4)
        def _(f):
            dech[f] = zrow

    @pl.when(jnp.logical_not(has_up))
    def _():
        @pl.loop(0, 6)
        def _(f):
            fv[f, 9] = zrow

    @pl.when(jnp.logical_not(has_prev))
    def _():
        @pl.loop(0, 2)
        def _(f):
            @pl.loop(0, 10)
            def _(h):
                fv[f, h] = zrow

        @pl.loop(0, 4)
        def _(j):
            qin[j] = jnp.zeros((256, 256), BF)

    for s in range(2):
        scr[s, 0:8] = jnp.zeros((8, 128), F32)
        scr[s, 520:528] = jnp.zeros((8, 128), F32)
    for t in range(3):
        wt[t, 1152:1536, 0:128] = jnp.zeros((384, 128), BF)
        wt[t, 0:384, 128:256] = jnp.zeros((384, 128), BF)

    for c in local:
        c.wait()

    def prep(f, h):
        half = 0.5 * fv[f, h].astype(F32)
        a = half + half * jnp.tanh(half)
        scr[0, 8:520] = a
        base = pl.multiple_of(h * 384, 128)
        act[f, :, pl.ds(base, 128)] = scr[0, 7:519].astype(BF)
        act[f, :, pl.ds(base + 128, 128)] = a.astype(BF)
        act[f, :, pl.ds(base + 256, 128)] = scr[0, 9:521].astype(BF)

    def cprep(f, h, d):
        scr[1, 8:520] = d.astype(F32)
        base = pl.multiple_of(h * 384, 128)
        cact[f, :, pl.ds(base, 128)] = scr[1, pl.ds(7, 256, stride=2)].astype(BF)
        cact[f, :, pl.ds(base + 128, 128)] = scr[1, pl.ds(8, 256, stride=2)].astype(BF)
        cact[f, :, pl.ds(base + 256, 128)] = scr[1, pl.ds(9, 256, stride=2)].astype(BF)

    def taps(first, p, which):
        lanes = pl.ds(pl.multiple_of(p * 768, 128), 1536)
        total = None
        for t in which:
            d = jnp.dot(act[first + t, :, lanes], wt[t], preferred_element_type=F32)
            total = d if total is None else total + d
        return total

    def out_copy(f, p):
        rows2 = pl.ds(p * 2, 2)
        return pltpu.make_async_copy(dec.at[f, rows2], out.at[f, rows2], osem.at[f, p])

    def finish(f, p, total):
        for o in range(2):
            h = 2 * p + o
            y = total[:, o * 128:(o + 1) * 128] + fv[f + 2, h + 1].astype(F32) + dbv[...]
            d = y.astype(BF)
            dec[f, h] = d
            cprep(f, h + 1, d)
        out_copy(f, p).start()

    def critic(f, t, j):
        lanes = pl.ds(pl.multiple_of(j * 768, 128), 1152)
        return jnp.dot(cact[f, :, lanes], cwv[t], preferred_element_type=F32)

    @pl.loop(3, 6)
    def _(f):
        @pl.loop(1, 9)
        def _(h):
            prep(f, h)

    @pl.when(has_up)
    def _():
        own_up.wait_send()
        own_dn_recv = remote(feat.at[:, 0], fv.at[pl.ds(2, 4), 9], dns.at[0], dnr.at[0], dn)
        own_dn_recv.wait_recv()

    @pl.when(has_dn)
    def _():
        own_dn.wait_send()
        own_up.wait_recv()

    @pl.loop(3, 6)
    def _(f):
        prep(f, 0)
        prep(f, 9)

    def decode(f):
        @pl.loop(0, 4)
        def _(i):
            p = 3 - i
            finish(f, p, taps(f, p, (0, 1, 2)))

        @pl.when(has_up)
        def _():
            decs[f].start()

    decode(3)

    @pl.when(has_prev)
    def _():
        feats[0].wait_recv()
        feats[1].wait_recv()

        @pl.when(has_up)
        def _():
            fwd_up.start()

        @pl.when(has_dn)
        def _():
            fwd_dn.start()

    @pl.loop(0, 10)
    def _(h):
        prep(2, h)

    decode(2)

    def halo_dec(f):
        @pl.when(has_dn)
        def _():
            decs[f].wait_recv()
        cprep(f, 0, dech[f])

    halo_dec(3)

    @pl.loop(0, 4)
    def _(j):
        qout[j] = critic(3, 0, j).astype(BF)

    @pl.when(has_next)
    def _():
        for c in quot:
            c.start()

    halo_dec(2)

    @pl.loop(0, 4)
    def _(j):
        cacc[1, j] = critic(2, 1, j) + critic(3, 2, j)

    @pl.loop(0, 4)
    def _(p):
        part[0, p] = taps(0, p, (2,))
        part[1, p] = taps(1, p, (1, 2))

    def arrived(k):
        @pl.when(has_prev)
        def _():
            feats[k].wait_recv()

    def prep2(h):
        prep(0, h)
        prep(1, h)

    prep2(8)
    prep2(1)

    @pl.when(jnp.logical_and(has_prev, has_up))
    def _():
        fwd_dn.wait_recv()

    prep2(9)

    @pl.when(jnp.logical_and(has_prev, has_dn))
    def _():
        fwd_up.wait_recv()

    prep2(0)

    def rest(p):
        finish(0, p, part[0, p] + taps(0, p, (0, 1)))
        finish(1, p, part[1, p] + taps(1, p, (0,)))

    for k, pairs in ((2, ()), (3, (3,)), (4, ()), (5, (2,)), (6, ()), (7, (1, 0))):
        arrived(k)
        prep2(ORDER[k] + 1)
        for p in pairs:
            rest(p)
            if p == 3:
                @pl.when(has_up)
                def _():
                    decs[0].start()
                    decs[1].start()

    halo_dec(0)
    halo_dec(1)

    def c_copy(c, j):
        return pltpu.make_async_copy(co.at[c, j], cout.at[c, j], csem.at[c, j])

    def leaky(v):
        return jnp.where(v > 0, v, 0.2 * v).astype(BF)

    @pl.loop(0, 4)
    def _(j):
        cacc[0, j] = critic(0, 1, j) + critic(1, 2, j)
        co[1, j] = leaky(cacc[1, j] + critic(1, 0, j) + cbv[...])
        c_copy(1, j).start()

    for j in range(4):
        @pl.when(has_prev)
        def _():
            quot[j].wait_recv()
        co[0, j] = leaky(cacc[0, j] + qin[j].astype(F32) + cbv[...])
        c_copy(0, j).start()

    @pl.when(has_next)
    def _():
        for c in feats:
            c.wait_send()
        for c in quot:
            c.wait_send()

    @pl.when(has_up)
    def _():
        for c in decs:
            c.wait_send()

    @pl.when(jnp.logical_and(has_prev, has_up))
    def _():
        fwd_up.wait_send()

    @pl.when(jnp.logical_and(has_prev, has_dn))
    def _():
        fwd_dn.wait_send()

    for f in range(4):
        for p in range(4):
            out_copy(f, p).wait()
    for c in range(2):
        for j in range(4):
            c_copy(c, j).wait()


def shards(features, decoder_weight, decoder_bias, critic_weight, critic_bias):
    V = pltpu.VMEM
    dma = pltpu.SemaphoreType.DMA
    anyspace = pl.BlockSpec(memory_space=pl.ANY)
    return pl.pallas_call(
        kernel,
        out_shape=(jax.ShapeDtypeStruct((4, 8, 512, 128), BF), jax.ShapeDtypeStruct((2, 4, 256, 256), BF)),
        in_specs=[anyspace] * 5,
        out_specs=(anyspace, anyspace),
        scratch_shapes=[
            V((6, 10, 512, 128), BF),
            V((6, 512, 3840), BF),
            V((3, 1536, 256), BF),
            V((3, 1152, 256), BF),
            V((1, 128), F32),
            V((1, 256), F32),
            V((4, 8, 512, 128), BF),
            V((4, 256, 3456), BF),
            V((4, 512, 128), BF),
            V((2, 4, 512, 256), F32),
            V((2, 4, 256, 256), F32),
            V((4, 256, 256), BF),
            V((4, 256, 256), BF),
            V((2, 4, 256, 256), BF),
            V((2, 528, 128), F32),
            dma((6,)), dma((4, 4)), dma((2, 4)),
            dma((8,)), dma((8,)), dma((4,)), dma((4,)),
            dma((6,)), dma((6,)), dma((2,)), dma((2,)),
        ],
        compiler_params=pltpu.CompilerParams(
            collective_id=0, has_side_effects=True, vmem_limit_bytes=62 << 20),
        cost_estimate=pl.CostEstimate(flops=40_000_000_000, bytes_accessed=20_000_000, transcendentals=4_000_000),
        name="tokenizer",
    )(
        features,
        decoder_weight.reshape(3, 1152, 128),
        decoder_bias.reshape(1, 128),
        critic_weight.reshape(3, 1152, 256),
        critic_bias.reshape(1, 256),
    )


def solution(mesh):
    in_specs = (P("tm", "rows", None, None), P(), P(), P(), P())
    out_specs = (P("tm", "rows", None, None), P("tm", "rows", None, None))
    return jax.shard_map(shards, mesh=mesh, in_specs=in_specs, out_specs=out_specs, check_vma=False)
```

```python
import jax
import jax.numpy as jnp
from jax import lax
from jax.experimental import pallas as pl
from jax.experimental.pallas import tpu as pltpu
from jax.sharding import PartitionSpec as P

MESH = pl.DeviceIdType.MESH
BF = jnp.bfloat16
F32 = jnp.float32
ORDER = (7, 0, 6, 5, 4, 3, 2, 1)


def kernel(feat, w, db, cw, cb, dec, co,
           fv, act, wt, cwv, dbv, cbv, cact, dech, part, cacc, qout, qin, scr,
           rbuf, rbs, rbr, loc, tms, tmr, qs, qr, ups, upr, dns, dnr):
    tm = lax.axis_index("tm")
    row = lax.axis_index("rows")
    n_tm = lax.axis_size("tm")
    n_row = lax.axis_size("rows")
    has_next = tm < n_tm - 1
    has_prev = tm > 0
    has_up = row < n_row - 1
    has_dn = row > 0
    nxt = (lax.rem(tm + 1, n_tm), row)
    prv = (lax.rem(tm + n_tm - 1, n_tm), row)
    up = (tm, lax.rem(row + 1, n_row))
    dn = (tm, lax.rem(row + n_row - 1, n_row))

    local = [
        pltpu.make_async_copy(feat, fv.at[pl.ds(2, 4), pl.ds(1, 8)], loc.at[0]),
        pltpu.make_async_copy(cw, cwv, loc.at[1]),
        pltpu.make_async_copy(w, wt.at[:, pl.ds(0, 1152), pl.ds(0, 128)], loc.at[2]),
        pltpu.make_async_copy(w, wt.at[:, pl.ds(384, 1152), pl.ds(128, 128)], loc.at[3]),
        pltpu.make_async_copy(db, dbv, loc.at[4]),
        pltpu.make_async_copy(cb, cbv, loc.at[5]),
    ]
    for c in local:
        c.start()

    mid = n_row // 2
    shed = ((0, 2, (3, 4)), (1, 6, (3,)), (n_row - 2, n_row - 3, (3,)), (n_row - 1, mid + 1, (3,)))

    barrier = pltpu.get_barrier_semaphore()
    count = 0
    pairs = [(has_next, nxt), (has_prev, prv), (has_up, up), (has_dn, dn)]
    for r, via, _ in shed:
        at_r, at_via = row == r, row == via
        pairs += [
            (jnp.logical_and(has_next, at_r), (nxt[0], via)),
            (jnp.logical_and(has_prev, at_r), (tm, via)),
            (jnp.logical_and(has_prev, at_via), (prv[0], r)),
            (jnp.logical_and(has_prev, at_via), (tm, r)),
        ]
    for ok, dev in pairs:
        @pl.when(ok)
        def _():
            pl.semaphore_signal(barrier, inc=1, device_id=dev, device_id_type=MESH)
        count = count + ok.astype(jnp.int32)
    pl.semaphore_wait(barrier, count)

    def remote(src, dst, ss, rs, dev):
        return pltpu.make_async_remote_copy(
            src_ref=src, dst_ref=dst, send_sem=ss, recv_sem=rs, device_id=dev, device_id_type=MESH)

    feats = [remote(feat.at[pl.ds(2, 2), h], fv.at[pl.ds(0, 2), h + 1], tms.at[k], tmr.at[k], nxt)
             for k, h in enumerate(ORDER)]
    own_up = remote(feat.at[:, 7], fv.at[pl.ds(2, 4), 0], ups.at[0], upr.at[0], up)
    own_dn = remote(feat.at[:, 0], fv.at[pl.ds(2, 4), 9], dns.at[0], dnr.at[0], dn)
    fwd_up = remote(fv.at[pl.ds(0, 2), 8], fv.at[pl.ds(0, 2), 0], ups.at[1], upr.at[1], up)
    fwd_dn = remote(fv.at[pl.ds(0, 2), 1], fv.at[pl.ds(0, 2), 9], dns.at[1], dnr.at[1], dn)
    decs = [remote(dec.at[f, 7], dech.at[f], ups.at[2 + f], upr.at[2 + f], up) for f in range(4)]
    quot = [remote(qout.at[j], qin.at[j], qs.at[j], qr.at[j], nxt) for j in range(4)]

    @pl.when(has_up)
    def _():
        own_up.start()

    @pl.when(has_dn)
    def _():
        own_dn.start()

    def detour(r, via, places, k):
        slot = places.index(k)
        return remote(feat.at[pl.ds(2, 2), ORDER[k]], rbuf.at[slot], tms.at[k], rbr.at[slot], (nxt[0], via))

    def onward(r, via, places, k):
        slot = places.index(k)
        return remote(rbuf.at[slot], fv.at[pl.ds(0, 2), ORDER[k] + 1], rbs.at[slot], tmr.at[k], (tm, r))

    for k in range(8):
        direct = has_next
        for r, via, places in shed:
            if k in places:
                direct = jnp.logical_and(direct, row != r)

                @pl.when(jnp.logical_and(has_next, row == r))
                def _():
                    detour(r, via, places, k).start()

        @pl.when(direct)
        def _():
            feats[k].start()

    zrow = jnp.zeros((512, 128), BF)

    @pl.when(jnp.logical_not(has_dn))
    def _():
        @pl.loop(0, 6)
        def _(f):
            fv[f, 0] = zrow

        @pl.loop(0, 4)
        def _(f):
            dech[f] = zrow

    @pl.when(jnp.logical_not(has_up))
    def _():
        @pl.loop(0, 6)
        def _(f):
            fv[f, 9] = zrow

    @pl.when(jnp.logical_not(has_prev))
    def _():
        @pl.loop(0, 2)
        def _(f):
            @pl.loop(0, 10)
            def _(h):
                fv[f, h] = zrow

        @pl.loop(0, 4)
        def _(j):
            qin[j] = jnp.zeros((256, 256), BF)

    for s in range(2):
        scr[s, 0:8] = jnp.zeros((8, 128), F32)
        scr[s, 520:528] = jnp.zeros((8, 128), F32)
    for t in range(3):
        wt[t, 1152:1536, 0:128] = jnp.zeros((384, 128), BF)
        wt[t, 0:384, 128:256] = jnp.zeros((384, 128), BF)

    for c in local:
        c.wait()

    def prep(f, h):
        half = 0.5 * fv[f, h].astype(F32)
        a = half + half * jnp.tanh(half)
        scr[0, 8:520] = a
        base = pl.multiple_of(h * 384, 128)
        act[f, :, pl.ds(base, 128)] = scr[0, 7:519].astype(BF)
        act[f, :, pl.ds(base + 128, 128)] = a.astype(BF)
        act[f, :, pl.ds(base + 256, 128)] = scr[0, 9:521].astype(BF)

    def cprep(f, h, d):
        scr[1, 8:520] = d.astype(F32)
        base = pl.multiple_of(h * 384, 128)
        cact[f, :, pl.ds(base, 128)] = scr[1, pl.ds(7, 256, stride=2)].astype(BF)
        cact[f, :, pl.ds(base + 128, 128)] = scr[1, pl.ds(8, 256, stride=2)].astype(BF)
        cact[f, :, pl.ds(base + 256, 128)] = scr[1, pl.ds(9, 256, stride=2)].astype(BF)

    def taps(first, p, which):
        lanes = pl.ds(pl.multiple_of(p * 768, 128), 1536)
        total = None
        for t in which:
            d = jnp.dot(act[first + t, :, lanes], wt[t], preferred_element_type=F32)
            total = d if total is None else total + d
        return total

    def finish(f, p, total):
        for o in range(2):
            h = 2 * p + o
            y = total[:, o * 128:(o + 1) * 128] + fv[f + 2, h + 1].astype(F32) + dbv[...]
            d = y.astype(BF)
            dec[f, h] = d
            cprep(f, h + 1, d)

    def critic(f, t, j):
        lanes = pl.ds(pl.multiple_of(j * 768, 128), 1152)
        return jnp.dot(cact[f, :, lanes], cwv[t], preferred_element_type=F32)

    @pl.loop(3, 6)
    def _(f):
        @pl.loop(1, 9)
        def _(h):
            prep(f, h)

    @pl.when(has_up)
    def _():
        own_up.wait_send()
        own_dn_recv = remote(feat.at[:, 0], fv.at[pl.ds(2, 4), 9], dns.at[0], dnr.at[0], dn)
        own_dn_recv.wait_recv()

    @pl.when(has_dn)
    def _():
        own_dn.wait_send()
        own_up.wait_recv()

    @pl.loop(3, 6)
    def _(f):
        prep(f, 0)
        prep(f, 9)

    def decode(f):
        @pl.loop(0, 4)
        def _(i):
            p = 3 - i
            finish(f, p, taps(f, p, (0, 1, 2)))

        @pl.when(has_up)
        def _():
            decs[f].start()

    decode(3)

    @pl.when(has_prev)
    def _():
        feats[0].wait_recv()
        feats[1].wait_recv()

        @pl.when(has_up)
        def _():
            fwd_up.start()

        @pl.when(has_dn)
        def _():
            fwd_dn.start()

    @pl.loop(0, 10)
    def _(h):
        prep(2, h)

    decode(2)

    def halo_dec(f):
        @pl.when(has_dn)
        def _():
            decs[f].wait_recv()
        cprep(f, 0, dech[f])

    halo_dec(3)

    @pl.loop(0, 4)
    def _(j):
        qout[j] = critic(3, 0, j).astype(BF)

    @pl.when(has_next)
    def _():
        for c in quot:
            c.start()

    halo_dec(2)

    @pl.loop(0, 4)
    def _(j):
        cacc[1, j] = critic(2, 1, j) + critic(3, 2, j)

    for r, via, places in shed:
        @pl.when(jnp.logical_and(has_prev, row == via))
        def _():
            for k in places:
                detour(r, via, places, k).wait_recv()
                onward(r, via, places, k).start()

    @pl.loop(0, 4)
    def _(p):
        part[0, p] = taps(0, p, (2,))
        part[1, p] = taps(1, p, (1, 2))

    def arrived(k):
        @pl.when(has_prev)
        def _():
            feats[k].wait_recv()

    def prep2(h):
        prep(0, h)
        prep(1, h)

    prep2(8)
    prep2(1)

    @pl.when(jnp.logical_and(has_prev, has_up))
    def _():
        fwd_dn.wait_recv()

    prep2(9)

    @pl.when(jnp.logical_and(has_prev, has_dn))
    def _():
        fwd_up.wait_recv()

    prep2(0)

    def rest(p):
        finish(0, p, part[0, p] + taps(0, p, (0, 1)))
        finish(1, p, part[1, p] + taps(1, p, (0,)))

    for k, pairs in ((2, ()), (3, (3,)), (4, ()), (5, (2,)), (6, ()), (7, (1, 0))):
        arrived(k)
        prep2(ORDER[k] + 1)
        for p in pairs:
            rest(p)
            if p == 3:
                @pl.when(has_up)
                def _():
                    decs[0].start()
                    decs[1].start()

    halo_dec(0)
    halo_dec(1)

    def leaky(v):
        return jnp.where(v > 0, v, 0.2 * v).astype(BF)

    @pl.loop(0, 4)
    def _(j):
        cacc[0, j] = critic(0, 1, j) + critic(1, 2, j)
        co[1, j] = leaky(cacc[1, j] + critic(1, 0, j) + cbv[...])

    for j in range(4):
        @pl.when(has_prev)
        def _():
            quot[j].wait_recv()
        co[0, j] = leaky(cacc[0, j] + qin[j].astype(F32) + cbv[...])

    for r, via, places in shed:
        @pl.when(jnp.logical_and(has_prev, row == via))
        def _():
            for k in places:
                onward(r, via, places, k).wait_send()

    @pl.when(has_next)
    def _():
        for c in feats:
            c.wait_send()
        for c in quot:
            c.wait_send()

    @pl.when(has_up)
    def _():
        for c in decs:
            c.wait_send()

    @pl.when(jnp.logical_and(has_prev, has_up))
    def _():
        fwd_up.wait_send()

    @pl.when(jnp.logical_and(has_prev, has_dn))
    def _():
        fwd_dn.wait_send()


def store(dec, co, out, cout, sems):
    copies = [pltpu.make_async_copy(dec.at[f], out.at[f], sems.at[f]) for f in range(4)]
    copies += [pltpu.make_async_copy(co.at[c], cout.at[c], sems.at[4 + c]) for c in range(2)]
    for c in copies:
        c.start()
    for c in copies:
        c.wait()


def shards(features, decoder_weight, decoder_bias, critic_weight, critic_bias):
    V = pltpu.VMEM
    dma = pltpu.SemaphoreType.DMA
    anyspace = pl.BlockSpec(memory_space=pl.ANY)
    results = pl.pallas_call(
        kernel,
        out_shape=(pltpu.VMEM((4, 8, 512, 128), BF), pltpu.VMEM((2, 4, 256, 256), BF)),
        in_specs=[anyspace] * 5,
        out_specs=(pl.BlockSpec(memory_space=pltpu.VMEM),) * 2,
        scratch_shapes=[
            V((6, 10, 512, 128), BF),
            V((6, 512, 3840), BF),
            V((3, 1536, 256), BF),
            V((3, 1152, 256), BF),
            V((1, 128), F32),
            V((1, 256), F32),
            V((4, 256, 3456), BF),
            V((4, 512, 128), BF),
            V((2, 4, 512, 256), F32),
            V((2, 4, 256, 256), F32),
            V((4, 256, 256), BF),
            V((4, 256, 256), BF),
            V((2, 528, 128), F32),
            V((2, 2, 512, 128), BF),
            dma((2,)), dma((2,)), dma((6,)),
            dma((8,)), dma((8,)), dma((4,)), dma((4,)),
            dma((6,)), dma((6,)), dma((2,)), dma((2,)),
        ],
        compiler_params=pltpu.CompilerParams(
            collective_id=0, has_side_effects=True, vmem_limit_bytes=54 << 20),
        cost_estimate=pl.CostEstimate(flops=40_000_000_000, bytes_accessed=20_000_000, transcendentals=4_000_000),
        name="tokenizer",
    )(
        features,
        decoder_weight.reshape(3, 1152, 128),
        decoder_bias.reshape(1, 128),
        critic_weight.reshape(3, 1152, 256),
        critic_bias.reshape(1, 256),
    )
    return pl.pallas_call(
        store,
        out_shape=(jax.ShapeDtypeStruct((4, 8, 512, 128), BF), jax.ShapeDtypeStruct((2, 4, 256, 256), BF)),
        in_specs=[anyspace] * 2,
        out_specs=(anyspace, anyspace),
        scratch_shapes=[dma((6,))],
        compiler_params=pltpu.CompilerParams(vmem_limit_bytes=1 << 20),
        name="store",
    )(*results)


def solution(mesh):
    in_specs = (P("tm", "rows", None, None), P(), P(), P(), P())
    out_specs = (P("tm", "rows", None, None), P("tm", "rows", None, None))
    return jax.shard_map(shards, mesh=mesh, in_specs=in_specs, out_specs=out_specs, check_vma=False)
```

```python
import jax
import jax.numpy as jnp
from jax import lax
from jax.experimental import pallas as pl
from jax.experimental.pallas import tpu as pltpu
from jax.sharding import PartitionSpec as P

MESH = pl.DeviceIdType.MESH
BF = jnp.bfloat16
F32 = jnp.float32
ORDER = (7, 0, 6, 5, 4, 3, 2, 1)


def kernel(feat, w, db, cw, cb, dec, co,
           fv, act, wt, cwv, dbv, cbv, cact, dech, part, cacc, qout, qin, scr,
           rbuf, rbs, rbr, loc, tms, tmr, qs, qr, ups, upr, dns, dnr):
    tm = lax.axis_index("tm")
    row = lax.axis_index("rows")
    n_tm = lax.axis_size("tm")
    n_row = lax.axis_size("rows")
    has_next = tm < n_tm - 1
    has_prev = tm > 0
    has_up = row < n_row - 1
    has_dn = row > 0
    nxt = (lax.rem(tm + 1, n_tm), row)
    prv = (lax.rem(tm + n_tm - 1, n_tm), row)
    up = (tm, lax.rem(row + 1, n_row))
    dn = (tm, lax.rem(row + n_row - 1, n_row))

    local = [
        pltpu.make_async_copy(feat, fv.at[pl.ds(2, 4), pl.ds(1, 8)], loc.at[0]),
        pltpu.make_async_copy(cw, cwv, loc.at[1]),
        pltpu.make_async_copy(w, wt.at[:, pl.ds(0, 1152), pl.ds(0, 128)], loc.at[2]),
        pltpu.make_async_copy(w, wt.at[:, pl.ds(384, 1152), pl.ds(128, 128)], loc.at[3]),
        pltpu.make_async_copy(db, dbv, loc.at[4]),
        pltpu.make_async_copy(cb, cbv, loc.at[5]),
    ]
    for c in local:
        c.start()

    mid = n_row // 2
    shed = ((0, 2, (3, 4)), (1, 6, (3,)), (n_row - 2, n_row - 3, (3,)), (n_row - 1, mid + 1, (3,)))

    barrier = pltpu.get_barrier_semaphore()
    count = 0
    pairs = [(has_next, nxt), (has_prev, prv), (has_up, up), (has_dn, dn)]
    for r, via, _ in shed:
        at_r, at_via = row == r, row == via
        pairs += [
            (jnp.logical_and(has_next, at_r), (nxt[0], via)),
            (jnp.logical_and(has_prev, at_r), (tm, via)),
            (jnp.logical_and(has_prev, at_via), (prv[0], r)),
            (jnp.logical_and(has_prev, at_via), (tm, r)),
        ]
    for ok, dev in pairs:
        @pl.when(ok)
        def _():
            pl.semaphore_signal(barrier, inc=1, device_id=dev, device_id_type=MESH)
        count = count + ok.astype(jnp.int32)
    pl.semaphore_wait(barrier, count)

    def remote(src, dst, ss, rs, dev):
        return pltpu.make_async_remote_copy(
            src_ref=src, dst_ref=dst, send_sem=ss, recv_sem=rs, device_id=dev, device_id_type=MESH)

    feats = [remote(feat.at[pl.ds(2, 2), h], fv.at[pl.ds(0, 2), h + 1], tms.at[k], tmr.at[k], nxt)
             for k, h in enumerate(ORDER)]
    own_up = remote(feat.at[:, 7], fv.at[pl.ds(2, 4), 0], ups.at[0], upr.at[0], up)
    own_dn = remote(feat.at[:, 0], fv.at[pl.ds(2, 4), 9], dns.at[0], dnr.at[0], dn)
    fwd_up = remote(fv.at[pl.ds(0, 2), 8], fv.at[pl.ds(0, 2), 0], ups.at[1], upr.at[1], up)
    fwd_dn = remote(fv.at[pl.ds(0, 2), 1], fv.at[pl.ds(0, 2), 9], dns.at[1], dnr.at[1], dn)
    decs = [remote(dec.at[f, 7], dech.at[f], ups.at[2 + f], upr.at[2 + f], up) for f in range(4)]
    quot = [remote(qout.at[j], qin.at[j], qs.at[j], qr.at[j], nxt) for j in range(4)]

    @pl.when(has_up)
    def _():
        own_up.start()

    @pl.when(has_dn)
    def _():
        own_dn.start()

    def detour(r, via, places, k):
        slot = places.index(k)
        return remote(feat.at[pl.ds(2, 2), ORDER[k]], rbuf.at[slot], tms.at[k], rbr.at[slot], (nxt[0], via))

    def onward(r, via, places, k):
        slot = places.index(k)
        return remote(rbuf.at[slot], fv.at[pl.ds(0, 2), ORDER[k] + 1], rbs.at[slot], tmr.at[k], (tm, r))

    for k in range(8):
        direct = has_next
        for r, via, places in shed:
            if k in places:
                direct = jnp.logical_and(direct, row != r)

                @pl.when(jnp.logical_and(has_next, row == r))
                def _():
                    detour(r, via, places, k).start()

        @pl.when(direct)
        def _():
            feats[k].start()

    zrow = jnp.zeros((512, 128), BF)

    @pl.when(jnp.logical_not(has_dn))
    def _():
        @pl.loop(0, 6)
        def _(f):
            fv[f, 0] = zrow

        @pl.loop(0, 4)
        def _(f):
            dech[f] = zrow

    @pl.when(jnp.logical_not(has_up))
    def _():
        @pl.loop(0, 6)
        def _(f):
            fv[f, 9] = zrow

    @pl.when(jnp.logical_not(has_prev))
    def _():
        @pl.loop(0, 2)
        def _(f):
            @pl.loop(0, 10)
            def _(h):
                fv[f, h] = zrow

        @pl.loop(0, 4)
        def _(j):
            qin[j] = jnp.zeros((256, 256), BF)

    for s in range(2):
        scr[s, 0:8] = jnp.zeros((8, 128), F32)
        scr[s, 520:528] = jnp.zeros((8, 128), F32)
    for t in range(3):
        wt[t, 1152:1536, 0:128] = jnp.zeros((384, 128), BF)
        wt[t, 0:384, 128:256] = jnp.zeros((384, 128), BF)

    for c in local:
        c.wait()

    def prep(f, h):
        half = 0.5 * fv[f, h].astype(F32)
        a = half + half * jnp.tanh(half)
        scr[0, 8:520] = a
        base = pl.multiple_of(h * 384, 128)
        act[f, :, pl.ds(base, 128)] = scr[0, 7:519].astype(BF)
        act[f, :, pl.ds(base + 128, 128)] = a.astype(BF)
        act[f, :, pl.ds(base + 256, 128)] = scr[0, 9:521].astype(BF)

    def cprep(f, h, d):
        scr[1, 8:520] = d.astype(F32)
        base = pl.multiple_of(h * 384, 128)
        cact[f, :, pl.ds(base, 128)] = scr[1, pl.ds(7, 256, stride=2)].astype(BF)
        cact[f, :, pl.ds(base + 128, 128)] = scr[1, pl.ds(8, 256, stride=2)].astype(BF)
        cact[f, :, pl.ds(base + 256, 128)] = scr[1, pl.ds(9, 256, stride=2)].astype(BF)

    def taps(first, p, which):
        lanes = pl.ds(pl.multiple_of(p * 768, 128), 1536)
        total = None
        for t in which:
            d = jnp.dot(act[first + t, :, lanes], wt[t], preferred_element_type=F32)
            total = d if total is None else total + d
        return total

    def finish(f, p, total):
        for o in range(2):
            h = 2 * p + o
            y = total[:, o * 128:(o + 1) * 128] + fv[f + 2, h + 1].astype(F32) + dbv[...]
            d = y.astype(BF)
            dec[f, h] = d
            cprep(f, h + 1, d)

    def critic(f, t, j):
        lanes = pl.ds(pl.multiple_of(j * 768, 128), 1152)
        return jnp.dot(cact[f, :, lanes], cwv[t], preferred_element_type=F32)

    @pl.loop(3, 6)
    def _(f):
        @pl.loop(1, 9)
        def _(h):
            prep(f, h)

    @pl.when(has_up)
    def _():
        own_up.wait_send()
        own_dn_recv = remote(feat.at[:, 0], fv.at[pl.ds(2, 4), 9], dns.at[0], dnr.at[0], dn)
        own_dn_recv.wait_recv()

    @pl.when(has_dn)
    def _():
        own_dn.wait_send()
        own_up.wait_recv()

    @pl.loop(3, 6)
    def _(f):
        prep(f, 0)
        prep(f, 9)

    def decode(f):
        @pl.loop(0, 4)
        def _(i):
            p = 3 - i
            finish(f, p, taps(f, p, (0, 1, 2)))

        @pl.when(has_up)
        def _():
            decs[f].start()

    decode(3)

    @pl.when(has_prev)
    def _():
        feats[0].wait_recv()
        feats[1].wait_recv()

        @pl.when(has_up)
        def _():
            fwd_up.start()

        @pl.when(has_dn)
        def _():
            fwd_dn.start()

    @pl.loop(0, 10)
    def _(h):
        prep(2, h)

    decode(2)

    def halo_dec(f):
        @pl.when(has_dn)
        def _():
            decs[f].wait_recv()
        cprep(f, 0, dech[f])

    halo_dec(3)

    @pl.loop(0, 4)
    def _(j):
        qout[j] = critic(3, 0, j).astype(BF)

    @pl.when(has_next)
    def _():
        for c in quot:
            c.start()

    halo_dec(2)

    @pl.loop(0, 4)
    def _(j):
        cacc[1, j] = critic(2, 1, j) + critic(3, 2, j)

    for r, via, places in shed:
        @pl.when(jnp.logical_and(has_prev, row == via))
        def _():
            for k in places:
                detour(r, via, places, k).wait_recv()
                onward(r, via, places, k).start()

    @pl.loop(0, 4)
    def _(p):
        part[0, p] = taps(0, p, (2,))
        part[1, p] = taps(1, p, (1, 2))

    def arrived(k):
        @pl.when(has_prev)
        def _():
            feats[k].wait_recv()

    def prep2(h):
        prep(0, h)
        prep(1, h)

    prep2(8)
    prep2(1)

    @pl.when(jnp.logical_and(has_prev, has_up))
    def _():
        fwd_dn.wait_recv()

    prep2(9)

    @pl.when(jnp.logical_and(has_prev, has_dn))
    def _():
        fwd_up.wait_recv()

    prep2(0)

    def rest(p):
        finish(0, p, part[0, p] + taps(0, p, (0, 1)))
        finish(1, p, part[1, p] + taps(1, p, (0,)))

    def leaky(v):
        return jnp.where(v > 0, v, 0.2 * v).astype(BF)

    def local_critic(j):
        cacc[0, j] = critic(0, 1, j) + critic(1, 2, j)
        co[1, j] = leaky(cacc[1, j] + critic(1, 0, j) + cbv[...])

    for k, pairs in ((2, ()), (3, (3,)), (4, ()), (5, (2,)), (6, ()), (7, (1, 0))):
        arrived(k)
        prep2(ORDER[k] + 1)
        for p in pairs:
            rest(p)
            if p < 3:
                local_critic(p + 1)
            if p == 3:
                @pl.when(has_up)
                def _():
                    decs[0].start()
                    decs[1].start()


    halo_dec(0)
    halo_dec(1)
    local_critic(0)

    for j in range(4):
        @pl.when(has_prev)
        def _():
            quot[j].wait_recv()
        co[0, j] = leaky(cacc[0, j] + qin[j].astype(F32) + cbv[...])

    for r, via, places in shed:
        @pl.when(jnp.logical_and(has_prev, row == via))
        def _():
            for k in places:
                onward(r, via, places, k).wait_send()

    @pl.when(has_next)
    def _():
        for c in feats:
            c.wait_send()
        for c in quot:
            c.wait_send()

    @pl.when(has_up)
    def _():
        for c in decs:
            c.wait_send()

    @pl.when(jnp.logical_and(has_prev, has_up))
    def _():
        fwd_up.wait_send()

    @pl.when(jnp.logical_and(has_prev, has_dn))
    def _():
        fwd_dn.wait_send()


def store(dec, co, out, cout, sems):
    copies = [pltpu.make_async_copy(dec.at[f], out.at[f], sems.at[f]) for f in range(4)]
    copies += [pltpu.make_async_copy(co.at[c], cout.at[c], sems.at[4 + c]) for c in range(2)]
    for c in copies:
        c.start()
    for c in copies:
        c.wait()


def shards(features, decoder_weight, decoder_bias, critic_weight, critic_bias):
    V = pltpu.VMEM
    dma = pltpu.SemaphoreType.DMA
    anyspace = pl.BlockSpec(memory_space=pl.ANY)
    results = pl.pallas_call(
        kernel,
        out_shape=(pltpu.VMEM((4, 8, 512, 128), BF), pltpu.VMEM((2, 4, 256, 256), BF)),
        in_specs=[anyspace] * 5,
        out_specs=(pl.BlockSpec(memory_space=pltpu.VMEM),) * 2,
        scratch_shapes=[
            V((6, 10, 512, 128), BF),
            V((6, 512, 3840), BF),
            V((3, 1536, 256), BF),
            V((3, 1152, 256), BF),
            V((1, 128), F32),
            V((1, 256), F32),
            V((4, 256, 3456), BF),
            V((4, 512, 128), BF),
            V((2, 4, 512, 256), F32),
            V((2, 4, 256, 256), F32),
            V((4, 256, 256), BF),
            V((4, 256, 256), BF),
            V((2, 528, 128), F32),
            V((2, 2, 512, 128), BF),
            dma((2,)), dma((2,)), dma((6,)),
            dma((8,)), dma((8,)), dma((4,)), dma((4,)),
            dma((6,)), dma((6,)), dma((2,)), dma((2,)),
        ],
        compiler_params=pltpu.CompilerParams(
            collective_id=0, has_side_effects=True, vmem_limit_bytes=54 << 20),
        cost_estimate=pl.CostEstimate(flops=40_000_000_000, bytes_accessed=20_000_000, transcendentals=4_000_000),
        name="tokenizer",
    )(
        features,
        decoder_weight.reshape(3, 1152, 128),
        decoder_bias.reshape(1, 128),
        critic_weight.reshape(3, 1152, 256),
        critic_bias.reshape(1, 256),
    )
    return pl.pallas_call(
        store,
        out_shape=(jax.ShapeDtypeStruct((4, 8, 512, 128), BF), jax.ShapeDtypeStruct((2, 4, 256, 256), BF)),
        in_specs=[anyspace] * 2,
        out_specs=(anyspace, anyspace),
        scratch_shapes=[dma((6,))],
        compiler_params=pltpu.CompilerParams(vmem_limit_bytes=1 << 20),
        name="store",
    )(*results)


def solution(mesh):
    in_specs = (P("tm", "rows", None, None), P(), P(), P(), P())
    out_specs = (P("tm", "rows", None, None), P("tm", "rows", None, None))
    return jax.shard_map(shards, mesh=mesh, in_specs=in_specs, out_specs=out_specs, check_vma=False)
```
